32 devices in a mesh: sec: 16 (over z, x, core), mpo: 2 (over y).
Axes of the slice: x: 2, y: 2, z: 4, core: 2. Of those that a mesh axis runs over, the one named last changes fastest.
Arguments:
- two_site: bfloat16 [256, 128, 128], P('sec'), may hold values from -6 to 6
- left_env: bfloat16 [64, 32, 128, 128], P('mpo', 'sec'), may hold values from -0.5 to 0.5
- right_env: bfloat16 [64, 32, 128, 128], P('mpo', 'sec'), may hold values from -0.5 to 0.5
- left_sector: int32 [256], P('sec'), may hold values from 0 to 31, as said below
- right_sector: int32 [256], P('sec'), may hold values from 0 to 31, as said below
- mpo_weight: float32 [64, 4], P('mpo'), may hold values from -0.75 to 0.75
- src_slot: int32 [256, 4], P('sec'), may hold values from 0 to 15
- joining: float32 [256, 4], P('sec'), may hold values from -4 to 4
Outputs:
- applied_state: bfloat16 [256, 128, 128], P('sec', 'mpo')
The draws below stay inside these ranges and needn't reach their ends.
Inputs may be any that keep to these rules, and one draw needn't show every extreme that they name: `left_sector`: block k's left sector is one held by the same index of sec as the block: between 2 * (k // 16) and that plus 2 - 1. `right_sector`: block k's right sector is one held by the same index of sec as the block: between 2 * (k // 16) and that plus 2 - 1.
All inputs are finite; a program needn't handle non-finite values.
Results may differ from the reference program's by a relative error of at most 0.0049.
Values sent between devices are 32-bit elements; how exact they have to be, the bound alone decides.
A program may use at most 64 MiB of HBM per device.

```python
import jax
import jax.numpy as jnp
from jax import lax

BLK = 128
WB = 64
CHAN = 4
NS_DEV = 2
NB_DEV = 16
NS = 32
NB = 256
N_SEC = 16


def sector_draw(key, salt):
    local = jax.random.randint(jax.random.fold_in(key, salt), (NB,), 0, NS_DEV)
    owner = jnp.arange(NB, dtype=jnp.int32) // NB_DEV
    return (owner * NS_DEV + local).astype(jnp.int32)


def draw_left_sector(key, part):
    return sector_draw(key, 11)


def draw_right_sector(key, part):
    return sector_draw(key, 23)


def touch_ends(entries, rng, least, high):
    dims = entries.shape
    place = [jax.random.randint(jax.random.fold_in(rng, axis), (), 0, dims[axis]) for axis in range(len(dims))]
    entries = entries.at[tuple(place)].set(least)
    longest = dims.index(max(dims))
    place[longest] = (place[longest] + 1) % dims[longest]
    return entries.at[tuple(place)].set(high)


def level_of(stream_key, dims, pieces, least, largest):
    def one(dim, shards_of):
        draws = jax.random.uniform(jax.random.fold_in(jax.random.fold_in(stream_key, 6), dim), (shards_of,), jnp.float32, least / len(pieces), largest / len(pieces))
        return jnp.repeat(jnp.exp(draws), dims[dim] // shards_of).reshape((-1,) + (1,) * (len(dims) - dim - 1))

    factor_of = one(*pieces[0])
    for cut in pieces[1:]:
        factor_of = factor_of * one(*cut)
    return factor_of


def normal_values(key, dims, spread, reach, shards=(), kind=jnp.bfloat16):
    values = jax.random.normal(key, dims, jnp.float32) * spread
    if len(shards) > 0:
        values = level_of(key, dims, shards, -0.22, 0.18) * values
    return jnp.clip(values, min=-reach, max=reach).astype(kind)


def setup_inputs(seed: int = 0) -> dict:
    streams_of = jax.random.split(jax.random.key(seed), 9)
    two_site = normal_values(streams_of[0], (NB, BLK, BLK), 1.0, 6.0, ((0, 16),))
    left_env = normal_values(streams_of[1], (WB, NS, BLK, BLK), BLK ** -0.5, 0.5, ((0, 2), (1, 16)))
    right_env = normal_values(streams_of[2], (WB, NS, BLK, BLK), BLK ** -0.5, 0.5, ((0, 2), (1, 16)))
    left_sector = draw_left_sector(jax.random.fold_in(streams_of[8], 71), 0)
    right_sector = draw_right_sector(jax.random.fold_in(streams_of[8], 71), 0)
    mpo_weight = normal_values(streams_of[5], (WB, CHAN), WB ** -0.5, 0.75, ((0, 2),), jnp.float32)
    src_slot = touch_ends(jax.random.randint(streams_of[6], (NB, CHAN), 0, NB_DEV), jax.random.fold_in(streams_of[6], 1), 0, NB_DEV - 1).astype(jnp.int32)
    joining = normal_values(streams_of[7], (NB, CHAN), 0.5, 4.0, ((0, 16),), jnp.float32)
    return {"two_site": two_site, "left_env": left_env, "right_env": right_env, "left_sector": left_sector, "right_sector": right_sector, "mpo_weight": mpo_weight, "src_slot": src_slot, "joining": joining}


def reference(two_site, left_env, right_env, left_sector, right_sector, mpo_weight, src_slot, joining):
    group = 8
    count = NB // group

    def one_group(items):
        blocks, left_ids, right_ids = items
        left_blocks = jnp.take(left_env, left_ids, axis=1).astype(jnp.float32)
        right_blocks = jnp.take(right_env, right_ids, axis=1).astype(jnp.float32)
        product = jnp.einsum("wgac,gcd->wgad", left_blocks, blocks.astype(jnp.float32)).astype(jnp.bfloat16)
        applied = jnp.einsum("wgad,wgbd->wgab", product.astype(jnp.float32), right_blocks)
        return jnp.einsum("wf,wgab->gfab", mpo_weight, applied, precision=lax.Precision.HIGHEST)

    grouped = (two_site.reshape(count, group, BLK, BLK), left_sector.reshape(count, group), right_sector.reshape(count, group))
    channel_sums = lax.map(one_group, grouped).reshape(NB, CHAN, BLK, BLK)
    owner = jnp.arange(NB, dtype=jnp.int32) // NB_DEV
    shifts = [0, -1, 1, -(N_SEC // 2)]
    summed = jnp.zeros((NB, BLK, BLK), jnp.float32)
    for channel in range(CHAN):
        source = ((owner + shifts[channel]) % N_SEC) * NB_DEV + src_slot[:, channel]
        picked = channel_sums[source.astype(jnp.int32), channel]
        summed = summed + joining[:, channel][:, None, None] * picked
    return summed.astype(jnp.bfloat16)
```

```python
import functools

import jax
import jax.numpy as jnp
from jax import lax
from jax.experimental import pallas as pl
from jax.experimental.pallas import tpu as pltpu
from jax.sharding import PartitionSpec as P

MESH = pl.DeviceIdType.MESH
NT = (((1,), (1,)), ((), ()))


def kernel(
    n_sec, n_mpo, kb, wg,
    two_ref, left_ref, right_ref, lsec_ref, rsec_ref, wt_ref, slot_ref, join_ref,
    out_ref,
    z_ref, p_ref, r_ref, cs_ref, lower_ref, upper_ref, y3_ref, c3_ref, opp_ref, part_ref, yp_ref,
    y3_send, y3_recv, c1_send, c1_recv, c2_send, c2_recv, c3_send, c3_recv, yp_send, yp_recv,
):
    blocks, blk, _ = two_ref.shape
    bonds, sectors = left_ref.shape[:2]
    channels = cs_ref.shape[0]
    rows = blk // n_mpo
    chunks = blocks // kb
    pieces = yp_send.shape[1]
    per = blocks // pieces
    sec = lax.axis_index("sec")
    mpo = lax.axis_index("mpo")
    after = lax.rem(sec + 1, n_sec)
    before = lax.rem(sec + n_sec - 1, n_sec)
    across = lax.rem(sec + n_sec // 2, n_sec)
    peers = [lax.rem(mpo + i, n_mpo) for i in range(1, n_mpo)]
    targets = [(after, mpo), (before, mpo), (across, mpo)] + [(sec, peer) for peer in peers]

    barrier = pltpu.get_barrier_semaphore()
    for target in targets:
        pl.semaphore_signal(barrier, inc=1, device_id=target, device_id_type=MESH)

    def scale(w, carry):
        for s in range(sectors):
            block = right_ref[w, s].astype(jnp.float32)
            for c in range(channels):
                r_ref[s, pl.ds(c * blk, blk), pl.ds(pl.multiple_of(w * blk, blk), blk)] = (
                    block * wt_ref[w, c]
                ).astype(jnp.bfloat16)
        return carry

    lax.fori_loop(0, bonds, scale, 0)
    pl.semaphore_wait(barrier, len(targets))

    def remote(src, dst, send, recv, target):
        return pltpu.make_async_remote_copy(
            src_ref=src, dst_ref=dst, send_sem=send, recv_sem=recv, device_id=target, device_id_type=MESH
        )

    def y3_copy(i, q):
        ks = pl.ds(q * kb, kb)
        cut = pl.ds(pl.multiple_of(peers[i] * rows, rows), rows)
        return remote(cs_ref.at[3, ks, cut], y3_ref.at[i, ks], y3_send.at[i, q], y3_recv.at[i, q], (sec, peers[i]))

    def c1_copy(q):
        ks = pl.ds(q * kb, kb)
        return remote(cs_ref.at[1, ks], lower_ref.at[ks], c1_send.at[q], c1_recv.at[q], (after, mpo))

    def c2_copy(q):
        ks = pl.ds(q * kb, kb)
        return remote(cs_ref.at[2, ks], upper_ref.at[ks], c2_send.at[q], c2_recv.at[q], (before, mpo))

    def c3_copy(q):
        ks = pl.ds(q * kb, kb)
        return remote(c3_ref.at[ks], opp_ref.at[ks], c3_send.at[q], c3_recv.at[q], (across, mpo))

    def yp_copy(i, t):
        ks = pl.ds(t * per, per)
        cut = pl.ds(pl.multiple_of(peers[i] * rows, rows), rows)
        return remote(part_ref.at[ks, cut], yp_ref.at[i, ks], yp_send.at[i, t], yp_recv.at[i, t], (sec, peers[i]))

    mine = pl.ds(pl.multiple_of(mpo * rows, rows), rows)

    def reduce_c3(q):
        ks = pl.ds(q * kb, kb)
        total = cs_ref[3, ks, mine]
        for i in range(n_mpo - 1):
            y3_copy(i, q).wait_recv()
            total = total + y3_ref[i, ks]
        c3_ref[ks] = total
        c3_copy(q).start()

    def chunk(q, carry):
        for j in range(kb):
            k = q * kb + j
            block = two_ref[k]
            which = lax.rem(lsec_ref[k], sectors)
            for s in range(sectors):
                keep = jnp.where(which == s, 1.0, 0.0)
                z_ref[pl.ds(s * blk, blk), pl.ds(j * blk, blk)] = (
                    block.astype(jnp.float32) * keep
                ).astype(jnp.bfloat16)

        def product(g, inner):
            ws = pl.ds(g * wg, wg)
            lhs = jnp.concatenate(
                [left_ref[ws, s].reshape(wg * blk, blk) for s in range(sectors)], axis=1
            )
            made = jnp.dot(lhs, z_ref[...], preferred_element_type=jnp.float32).astype(jnp.bfloat16)
            for u in range(wg):
                place = pl.ds(pl.multiple_of((g * wg + u) * blk, blk), blk)
                for j in range(kb):
                    p_ref[j, :, place] = made[u * blk:(u + 1) * blk, j * blk:(j + 1) * blk]
            return inner

        lax.fori_loop(0, bonds // wg, product, 0)
        for j in range(kb):
            k = q * kb + j
            sums = lax.dot_general(
                p_ref[j], r_ref[lax.rem(rsec_ref[k], sectors)], NT, preferred_element_type=jnp.float32
            )
            for c in range(channels):
                cs_ref[c, k] = sums[:, c * blk:(c + 1) * blk]
        for i in range(n_mpo - 1):
            y3_copy(i, q).start()
        c1_copy(q).start()
        c2_copy(q).start()

        @pl.when(q >= 1)
        def _():
            reduce_c3(q - 1)

        return carry

    lax.fori_loop(0, chunks, chunk, 0)
    reduce_c3(chunks - 1)

    def arrived(q, carry):
        c1_copy(q).wait_recv()
        c2_copy(q).wait_recv()
        return carry

    lax.fori_loop(0, chunks, arrived, 0)

    def joined(t, carry):
        for j in range(per):
            k = t * per + j
            part_ref[k] = (
                join_ref[k, 0] * cs_ref[0, slot_ref[k, 0]]
                + join_ref[k, 1] * lower_ref[slot_ref[k, 1]]
                + join_ref[k, 2] * upper_ref[slot_ref[k, 2]]
            )
        for i in range(n_mpo - 1):
            yp_copy(i, t).start()
        return carry

    lax.fori_loop(0, pieces, joined, 0)

    def landed(q, carry):
        c3_copy(q).wait_recv()
        return carry

    lax.fori_loop(0, chunks, landed, 0)

    def finish(t, carry):
        for i in range(n_mpo - 1):
            yp_copy(i, t).wait_recv()
        for j in range(per):
            k = t * per + j
            total = part_ref[k, mine]
            for i in range(n_mpo - 1):
                total = total + yp_ref[i, k]
            total = total + join_ref[k, 3] * opp_ref[slot_ref[k, 3]]
            out_ref[k] = total.astype(out_ref.dtype)
        for i in range(n_mpo - 1):
            yp_copy(i, t).wait_send()
        return carry

    lax.fori_loop(0, pieces, finish, 0)

    def sent(q, carry):
        for i in range(n_mpo - 1):
            y3_copy(i, q).wait_send()
        c1_copy(q).wait_send()
        c2_copy(q).wait_send()
        c3_copy(q).wait_send()
        return carry

    lax.fori_loop(0, chunks, sent, 0)


def per_device(n_sec, n_mpo, two_site, left_env, right_env, *small):
    blocks, blk, _ = two_site.shape
    bonds, sectors = left_env.shape[:2]
    channels = small[2].shape[1]
    rows = blk // n_mpo
    kb = 2
    chunks = blocks // kb
    wg = min(bonds, 8)
    pieces = 4
    peers = n_mpo - 1
    vmem = pl.BlockSpec(memory_space=pltpu.VMEM)
    smem = pl.BlockSpec(memory_space=pltpu.SMEM)
    dma = pltpu.SemaphoreType.DMA
    f32, bf16 = jnp.float32, jnp.bfloat16
    return pl.pallas_call(
        functools.partial(kernel, n_sec, n_mpo, kb, wg),
        out_shape=jax.ShapeDtypeStruct((blocks, rows, blk), bf16),
        in_specs=[vmem] * 3 + [smem] * 5,
        out_specs=vmem,
        scratch_shapes=[
            pltpu.VMEM((sectors * blk, kb * blk), bf16),
            pltpu.VMEM((kb, blk, bonds * blk), bf16),
            pltpu.VMEM((sectors, channels * blk, bonds * blk), bf16),
            pltpu.VMEM((channels, blocks, blk, blk), f32),
            pltpu.VMEM((blocks, blk, blk), f32),
            pltpu.VMEM((blocks, blk, blk), f32),
            pltpu.VMEM((peers, blocks, rows, blk), f32),
            pltpu.VMEM((blocks, rows, blk), f32),
            pltpu.VMEM((blocks, rows, blk), f32),
            pltpu.VMEM((blocks, blk, blk), f32),
            pltpu.VMEM((peers, blocks, rows, blk), f32),
            dma((peers, chunks)), dma((peers, chunks)),
            dma((chunks,)), dma((chunks,)),
            dma((chunks,)), dma((chunks,)),
            dma((chunks,)), dma((chunks,)),
            dma((peers, pieces)), dma((peers, pieces)),
        ],
        compiler_params=pltpu.CompilerParams(
            collective_id=0, has_side_effects=True, vmem_limit_bytes=48 * 1024 * 1024
        ),
    )(two_site, left_env, right_env, *small)


def solution(mesh):
    placed = (
        P("sec", None, None),
        P("mpo", "sec", None, None),
        P("mpo", "sec", None, None),
        P("sec"),
        P("sec"),
        P("mpo", None),
        P("sec", None),
        P("sec", None),
    )
    return jax.shard_map(
        functools.partial(per_device, mesh.shape["sec"], mesh.shape["mpo"]),
        mesh=mesh, in_specs=placed, out_specs=P("sec", "mpo", None), check_vma=False,
    )
```

```python
import functools

import jax
import jax.numpy as jnp
from jax import lax
from jax.experimental import pallas as pl
from jax.experimental.pallas import tpu as pltpu
from jax.sharding import PartitionSpec as P

MESH = pl.DeviceIdType.MESH
PIECES = 4
LAG = 3


def kernel(
    n_sec, n_mpo, kb, wg,
    two_hbm, left_hbm, right_hbm, lsec_ref, rsec_ref, wt_ref, slot_ref, join_ref,
    out_ref,
    two_ref, left_ref, right_ref, z_ref, p_ref, far_r, near_r, far_ref, near_ref,
    y_ref, sum_ref, cross_ref, opp_ref, inner_ref, part_ref, yp_ref,
    in_sem, y_send, y_recv, x_send, x_recv, o_send, o_recv, n_send, n_recv, yp_send, yp_recv,
):
    blocks, blk, _ = two_ref.shape
    bonds, sectors = left_ref.shape[:2]
    rows = blk // n_mpo
    chunks = blocks // kb
    pieces = yp_send.shape[1]
    per = blocks // pieces
    cut_w = bonds // PIECES
    sec = lax.axis_index("sec")
    mpo = lax.axis_index("mpo")
    odd = lax.rem(sec, 2)
    partner = sec + 1 - 2 * odd
    crossing = lax.rem(sec + n_sec - 1 + 2 * odd, n_sec)
    across = lax.rem(sec + n_sec // 2, n_sec)
    out_channel = 2 - odd
    in_channel = 1 + odd
    peers = [lax.rem(mpo + i, n_mpo) for i in range(1, n_mpo)]
    targets = [(partner, mpo), (crossing, mpo), (across, mpo)] + [(sec, peer) for peer in peers]

    def right_copy(t):
        ws = pl.ds(t * cut_w, cut_w)
        return pltpu.make_async_copy(right_hbm.at[ws], right_ref.at[ws], in_sem.at[t])

    left_copy = pltpu.make_async_copy(left_hbm, left_ref, in_sem.at[PIECES])
    two_copy = pltpu.make_async_copy(two_hbm, two_ref, in_sem.at[PIECES + 1])
    for t in range(PIECES):
        right_copy(t).start()
    two_copy.start()
    left_copy.start()

    barrier = pltpu.get_barrier_semaphore()
    for target in targets:
        pl.semaphore_signal(barrier, inc=1, device_id=target, device_id_type=MESH)

    def scale(held, pair):
        def one(w, carry):
            for s in range(sectors):
                block = right_ref[w, s].T.astype(jnp.float32)
                for c in range(2):
                    held[s, pl.ds(pl.multiple_of(w * blk, blk), blk), c * blk:(c + 1) * blk] = (
                        block * wt_ref[pair[c], w]
                    ).astype(jnp.bfloat16)
            return carry

        return one

    far = scale(far_r, (out_channel, 3))
    near = scale(near_r, (0, in_channel))
    for t in range(PIECES):
        right_copy(t).wait()
        lax.fori_loop(t * cut_w, (t + 1) * cut_w, far, 0)
    two_copy.wait()
    left_copy.wait()
    pl.semaphore_wait(barrier, len(targets))

    def remote(src, dst, send, recv, target):
        return pltpu.make_async_remote_copy(
            src_ref=src, dst_ref=dst, send_sem=send, recv_sem=recv, device_id=target, device_id_type=MESH
        )

    def peer_rows(i):
        return pl.ds(pl.multiple_of(peers[i] * rows, rows), rows)

    def y_copy(i, q):
        ks = pl.ds(q * kb, kb)
        return remote(
            far_ref.at[:, ks, peer_rows(i)], y_ref.at[i, :, ks], y_send.at[i, q], y_recv.at[i, q], (sec, peers[i])
        )

    def x_copy(q):
        ks = pl.ds(q * kb, kb)
        return remote(sum_ref.at[0, ks], cross_ref.at[ks], x_send.at[q], x_recv.at[q], (crossing, mpo))

    def o_copy(q):
        ks = pl.ds(q * kb, kb)
        return remote(sum_ref.at[1, ks], opp_ref.at[ks], o_send.at[q], o_recv.at[q], (across, mpo))

    def n_copy(q):
        ks = pl.ds(q * kb, kb)
        return remote(near_ref.at[1, ks], inner_ref.at[ks], n_send.at[q], n_recv.at[q], (partner, mpo))

    def yp_copy(i, t):
        ks = pl.ds(t * per, per)
        return remote(
            part_ref.at[ks, peer_rows(i)], yp_ref.at[i, ks], yp_send.at[i, t], yp_recv.at[i, t], (sec, peers[i])
        )

    mine = pl.ds(pl.multiple_of(mpo * rows, rows), rows)

    def reduce(q):
        ks = pl.ds(q * kb, kb)
        total = far_ref[:, ks, mine]
        for i in range(n_mpo - 1):
            y_copy(i, q).wait_recv()
            total = total + y_ref[i, :, ks]
        sum_ref[:, ks] = total
        o_copy(q).start()
        x_copy(q).start()

    def multiply(held, sums_ref, k):
        sums = jnp.dot(p_ref[k], held[lax.rem(rsec_ref[k], sectors)], preferred_element_type=jnp.float32)
        for c in range(2):
            sums_ref[c, k] = sums[:, c * blk:(c + 1) * blk]

    def first(q, carry):
        for j in range(kb):
            k = q * kb + j
            block = two_ref[k].astype(jnp.float32)
            which = lax.rem(lsec_ref[k], sectors)
            for s in range(sectors):
                keep = jnp.where(which == s, 1.0, 0.0)
                z_ref[pl.ds(s * blk, blk), pl.ds(j * blk, blk)] = (block * keep).astype(jnp.bfloat16)

        def product(g, inner):
            ws = pl.ds(g * wg, wg)
            lhs = jnp.concatenate(
                [left_ref[ws, s].reshape(wg * blk, blk) for s in range(sectors)], axis=1
            )
            made = jnp.dot(lhs, z_ref[...], preferred_element_type=jnp.float32).astype(jnp.bfloat16)
            for u in range(wg):
                place = pl.ds(pl.multiple_of((g * wg + u) * blk, blk), blk)
                for j in range(kb):
                    p_ref[q * kb + j, :, place] = made[u * blk:(u + 1) * blk, j * blk:(j + 1) * blk]
            return inner

        lax.fori_loop(0, bonds // wg, product, 0)
        for j in range(kb):
            multiply(far_r, far_ref, q * kb + j)
        for i in range(n_mpo - 1):
            y_copy(i, q).start()

        @pl.when(q >= LAG)
        def _():
            reduce(q - LAG)

        return carry

    lax.fori_loop(0, chunks, first, 0)
    lax.fori_loop(0, bonds, near, 0)
    reduce(chunks - LAG)

    def second(q, carry):
        for j in range(kb):
            multiply(near_r, near_ref, q * kb + j)
        n_copy(q).start()
        return carry

    lax.fori_loop(0, chunks // 2, second, 0)
    for t in range(1, LAG - 1):
        reduce(chunks - LAG + t)
    lax.fori_loop(chunks // 2, chunks, second, 0)

    def arrived(q, carry):
        n_copy(q).wait_recv()
        return carry

    lax.fori_loop(0, chunks, arrived, 0)

    def joined(t, carry):
        for j in range(per):
            k = t * per + j
            part_ref[k] = (
                join_ref[0, k] * near_ref[0, slot_ref[0, k]]
                + join_ref[out_channel, k] * inner_ref[slot_ref[out_channel, k]]
            )
        for i in range(n_mpo - 1):
            yp_copy(i, t).start()
        return carry

    lax.fori_loop(0, pieces, joined, 0)
    reduce(chunks - 1)

    def landed(q, carry):
        o_copy(q).wait_recv()
        x_copy(q).wait_recv()
        return carry

    lax.fori_loop(0, chunks, landed, 0)

    def finish(t, carry):
        for i in range(n_mpo - 1):
            yp_copy(i, t).wait_recv()
        for j in range(per):
            k = t * per + j
            total = part_ref[k, mine]
            for i in range(n_mpo - 1):
                total = total + yp_ref[i, k]
            total = total + join_ref[in_channel, k] * cross_ref[slot_ref[in_channel, k]]
            total = total + join_ref[3, k] * opp_ref[slot_ref[3, k]]
            out_ref[k] = total.astype(out_ref.dtype)
        for i in range(n_mpo - 1):
            yp_copy(i, t).wait_send()
        return carry

    lax.fori_loop(0, pieces, finish, 0)

    def sent(q, carry):
        for i in range(n_mpo - 1):
            y_copy(i, q).wait_send()
        n_copy(q).wait_send()
        x_copy(q).wait_send()
        o_copy(q).wait_send()
        return carry

    lax.fori_loop(0, chunks, sent, 0)


def per_device(
    n_sec, n_mpo, two_site, left_env, right_env, left_sector, right_sector, mpo_weight, src_slot, joining
):
    blocks, blk, _ = two_site.shape
    bonds, sectors = left_env.shape[:2]
    rows = blk // n_mpo
    kb = 2
    chunks = blocks // kb
    wg = min(bonds, 8)
    pieces = 4
    peers = n_mpo - 1
    smem = pl.BlockSpec(memory_space=pltpu.SMEM)
    dma = pltpu.SemaphoreType.DMA
    f32, bf16 = jnp.float32, jnp.bfloat16
    return pl.pallas_call(
        functools.partial(kernel, n_sec, n_mpo, kb, wg),
        out_shape=jax.ShapeDtypeStruct((blocks, rows, blk), bf16),
        in_specs=[pl.BlockSpec(memory_space=pltpu.HBM)] * 3 + [smem] * 5,
        out_specs=pl.BlockSpec(memory_space=pltpu.VMEM),
        scratch_shapes=[
            pltpu.VMEM(two_site.shape, bf16),
            pltpu.VMEM(left_env.shape, bf16),
            pltpu.VMEM(right_env.shape, bf16),
            pltpu.VMEM((sectors * blk, kb * blk), bf16),
            pltpu.VMEM((blocks, blk, bonds * blk), bf16),
            pltpu.VMEM((sectors, bonds * blk, 2 * blk), bf16),
            pltpu.VMEM((sectors, bonds * blk, 2 * blk), bf16),
            pltpu.VMEM((2, blocks, blk, blk), f32),
            pltpu.VMEM((2, blocks, blk, blk), f32),
            pltpu.VMEM((peers, 2, blocks, rows, blk), f32),
            pltpu.VMEM((2, blocks, rows, blk), f32),
            pltpu.VMEM((blocks, rows, blk), f32),
            pltpu.VMEM((blocks, rows, blk), f32),
            pltpu.VMEM((blocks, blk, blk), f32),
            pltpu.VMEM((blocks, blk, blk), f32),
            pltpu.VMEM((peers, blocks, rows, blk), f32),
            dma((PIECES + 2,)),
            dma((peers, chunks)), dma((peers, chunks)),
            dma((chunks,)), dma((chunks,)),
            dma((chunks,)), dma((chunks,)),
            dma((chunks,)), dma((chunks,)),
            dma((peers, pieces)), dma((peers, pieces)),
        ],
        compiler_params=pltpu.CompilerParams(
            collective_id=0, has_side_effects=True, vmem_limit_bytes=56 * 1024 * 1024
        ),
    )(two_site, left_env, right_env, left_sector, right_sector, mpo_weight.T, src_slot.T, joining.T)


def solution(mesh):
    placed = (
        P("sec", None, None),
        P("mpo", "sec", None, None),
        P("mpo", "sec", None, None),
        P("sec"),
        P("sec"),
        P("mpo", None),
        P("sec", None),
        P("sec", None),
    )
    return jax.shard_map(
        functools.partial(per_device, mesh.shape["sec"], mesh.shape["mpo"]),
        mesh=mesh, in_specs=placed, out_specs=P("sec", "mpo", None), check_vma=False,
    )
```

```python
import functools

import jax
import jax.numpy as jnp
from jax import lax
from jax.experimental import pallas as pl
from jax.experimental.pallas import tpu as pltpu
from jax.sharding import PartitionSpec as P

MESH = pl.DeviceIdType.MESH
PIECES = 4
LAG = 3


def kernel(
    n_sec, n_mpo, kb, wg,
    two_hbm, left_hbm, right_hbm, lsec_ref, rsec_ref, wt_ref, slot_ref, join_ref,
    out_ref,
    two_ref, left_ref, right_ref, z_ref, p_ref, far_r, near_r, far_ref, near_ref,
    y_ref, sum_ref, cross_ref, opp_ref, inner_ref, wide_ref, part_ref, yp_ref,
    in_sem, y_send, y_recv, d_send, d_recv, w_send, w_recv, x_send, x_recv, o_send, o_recv, n_send, n_recv, yp_send, yp_recv,
):
    blocks, blk, _ = two_ref.shape
    bonds, sectors = left_ref.shape[:2]
    rows = blk // n_mpo
    chunks = blocks // kb
    pieces = yp_send.shape[1]
    per = blocks // pieces
    cut_w = bonds // PIECES
    sec = lax.axis_index("sec")
    mpo = lax.axis_index("mpo")
    odd = lax.rem(sec, 2)
    partner = sec + 1 - 2 * odd
    crossing = lax.rem(sec + n_sec - 1 + 2 * odd, n_sec)
    across = lax.rem(sec + n_sec // 2, n_sec)
    out_channel = 2 - odd
    beside = lax.rem(lax.div(sec, 2) + odd, 2) == 1
    apart = jnp.logical_not(beside)
    in_channel = 1 + odd
    peers = [lax.rem(mpo + i, n_mpo) for i in range(1, n_mpo)]
    targets = [(partner, mpo), (crossing, mpo), (across, mpo)] + [(sec, peer) for peer in peers]

    def right_copy(t):
        ws = pl.ds(t * cut_w, cut_w)
        return pltpu.make_async_copy(right_hbm.at[ws], right_ref.at[ws], in_sem.at[t])

    left_copy = pltpu.make_async_copy(left_hbm, left_ref, in_sem.at[PIECES])
    two_copy = pltpu.make_async_copy(two_hbm, two_ref, in_sem.at[PIECES + 1])
    for t in range(PIECES):
        right_copy(t).start()
    two_copy.start()
    left_copy.start()

    barrier = pltpu.get_barrier_semaphore()
    for target in targets:
        pl.semaphore_signal(barrier, inc=1, device_id=target, device_id_type=MESH)

    def scale(held, pair, w):
        for s in range(sectors):
            block = right_ref[w, s].T.astype(jnp.float32)
            for c in range(2):
                held[s, pl.ds(pl.multiple_of(w * blk, blk), blk), c * blk:(c + 1) * blk] = (
                    block * wt_ref[pair[c], w]
                ).astype(jnp.bfloat16)

    for t in range(PIECES):
        right_copy(t).wait()
    two_copy.wait()
    left_copy.wait()
    pl.semaphore_wait(barrier, len(targets))

    def remote(src, dst, send, recv, target):
        return pltpu.make_async_remote_copy(
            src_ref=src, dst_ref=dst, send_sem=send, recv_sem=recv, device_id=target, device_id_type=MESH
        )

    def peer_rows(i):
        return pl.ds(pl.multiple_of(peers[i] * rows, rows), rows)

    def y_copy(i, q):
        ks = pl.ds(q * kb, kb)
        return remote(
            far_ref.at[1, ks, peer_rows(i)], y_ref.at[i, 1, ks], y_send.at[i, q], y_recv.at[i, q], (sec, peers[i])
        )

    def d_copy(i, q):
        ks = pl.ds(q * kb, kb)
        return remote(
            far_ref.at[0, ks, peer_rows(i)], y_ref.at[i, 0, ks], d_send.at[i, q], d_recv.at[i, q], (sec, peers[i])
        )

    def w_copy(q):
        ks = pl.ds(q * kb, kb)
        return remote(far_ref.at[0, ks], wide_ref.at[ks], w_send.at[q], w_recv.at[q], (crossing, mpo))

    def x_copy(q):
        ks = pl.ds(q * kb, kb)
        return remote(sum_ref.at[0, ks], cross_ref.at[ks], x_send.at[q], x_recv.at[q], (crossing, mpo))

    def o_copy(q):
        ks = pl.ds(q * kb, kb)
        return remote(sum_ref.at[1, ks], opp_ref.at[ks], o_send.at[q], o_recv.at[q], (across, mpo))

    def n_copy(q):
        ks = pl.ds(q * kb, kb)
        return remote(near_ref.at[1, ks], inner_ref.at[ks], n_send.at[q], n_recv.at[q], (partner, mpo))

    def yp_copy(i, t):
        ks = pl.ds(t * per, per)
        return remote(
            part_ref.at[ks, peer_rows(i)], yp_ref.at[i, ks], yp_send.at[i, t], yp_recv.at[i, t], (sec, peers[i])
        )

    mine = pl.ds(pl.multiple_of(mpo * rows, rows), rows)

    def reduce(q):
        ks = pl.ds(q * kb, kb)
        total = far_ref[1, ks, mine]
        for i in range(n_mpo - 1):
            y_copy(i, q).wait_recv()
            total = total + y_ref[i, 1, ks]
        sum_ref[1, ks] = total
        o_copy(q).start()

        @pl.when(apart)
        def _():
            moved = far_ref[0, ks, mine]
            for i in range(n_mpo - 1):
                d_copy(i, q).wait_recv()
                moved = moved + y_ref[i, 0, ks]
            sum_ref[0, ks] = moved
            x_copy(q).start()

    def multiply(held, sums_ref, k):
        sums = jnp.dot(p_ref[k], held[lax.rem(rsec_ref[k], sectors)], preferred_element_type=jnp.float32)
        for c in range(2):
            sums_ref[c, k] = sums[:, c * blk:(c + 1) * blk]

    groups = bonds // wg
    spread = bonds // (groups * chunks)

    def first(q, fresh):
        for j in range(kb):
            k = q * kb + j
            block = two_ref[k].astype(jnp.float32)
            which = lax.rem(lsec_ref[k], sectors)
            for s in range(sectors):
                keep = jnp.where(which == s, 1.0, 0.0)
                z_ref[pl.ds(s * blk, blk), pl.ds(j * blk, blk)] = (block * keep).astype(jnp.bfloat16)

        def product(g, inner):
            for u in range(0, wg, 1):
                ws = pl.ds(g * wg + u, 1)
                lhs = jnp.concatenate(
                    [left_ref[ws, s].reshape(1 * blk, blk) for s in range(sectors)], axis=1
                )
                made = jnp.dot(lhs, z_ref[...], preferred_element_type=jnp.float32).astype(jnp.bfloat16)
                for v in range(1):
                    place = pl.ds(pl.multiple_of((g * wg + u + v) * blk, blk), blk)
                    for j in range(kb):
                        p_ref[q * kb + j, :, place] = made[v * blk:(v + 1) * blk, j * blk:(j + 1) * blk]
                if fresh:
                    for v in range(1):
                        scale(far_r, (out_channel, 3), g * wg + u + v)
            for v in range(spread):
                scale(near_r, (0, in_channel), (q * groups + g) * spread + v)
            return inner

        lax.fori_loop(0, groups, product, 0)
        for j in range(kb):
            multiply(far_r, far_ref, q * kb + j)
        for i in range(n_mpo - 1):
            y_copy(i, q).start()

        @pl.when(beside)
        def _():
            w_copy(q).start()

        @pl.when(apart)
        def _():
            for i in range(n_mpo - 1):
                d_copy(i, q).start()

    def later(q, carry):
        first(q, False)

        @pl.when(q >= LAG)
        def _():
            reduce(q - LAG)

        return carry

    first(0, True)
    lax.fori_loop(1, chunks, later, 0)
    reduce(chunks - LAG)

    def second(q, carry):
        for j in range(kb):
            multiply(near_r, near_ref, q * kb + j)
        n_copy(q).start()
        return carry

    lax.fori_loop(0, chunks // 2, second, 0)
    for t in range(1, LAG - 1):
        reduce(chunks - LAG + t)
    lax.fori_loop(chunks // 2, chunks, second, 0)

    def arrived(q, carry):
        n_copy(q).wait_recv()

        @pl.when(beside)
        def _():
            w_copy(q).wait_recv()

        return carry

    lax.fori_loop(0, chunks, arrived, 0)

    def joined(t, carry):
        for j in range(per):
            k = t * per + j
            part_ref[k] = (
                join_ref[0, k] * near_ref[0, slot_ref[0, k]]
                + join_ref[out_channel, k] * inner_ref[slot_ref[out_channel, k]]
            )

        @pl.when(beside)
        def _():
            for j in range(per):
                k = t * per + j
                part_ref[k] = part_ref[k] + join_ref[in_channel, k] * wide_ref[slot_ref[in_channel, k]]

        for i in range(n_mpo - 1):
            yp_copy(i, t).start()
        return carry

    lax.fori_loop(0, pieces, joined, 0)
    reduce(chunks - 1)

    def landed(q, carry):
        o_copy(q).wait_recv()

        @pl.when(apart)
        def _():
            x_copy(q).wait_recv()

        return carry

    lax.fori_loop(0, chunks, landed, 0)

    def finish(t, carry):
        for i in range(n_mpo - 1):
            yp_copy(i, t).wait_recv()

        def write(crossed):
            for j in range(per):
                k = t * per + j
                total = part_ref[k, mine]
                for i in range(n_mpo - 1):
                    total = total + yp_ref[i, k]
                if crossed:
                    total = total + join_ref[in_channel, k] * cross_ref[slot_ref[in_channel, k]]
                total = total + join_ref[3, k] * opp_ref[slot_ref[3, k]]
                out_ref[k] = total.astype(out_ref.dtype)

        @pl.when(apart)
        def _():
            write(True)

        @pl.when(beside)
        def _():
            write(False)

        for i in range(n_mpo - 1):
            yp_copy(i, t).wait_send()
        return carry

    lax.fori_loop(0, pieces, finish, 0)

    def sent(q, carry):
        for i in range(n_mpo - 1):
            y_copy(i, q).wait_send()
        n_copy(q).wait_send()
        o_copy(q).wait_send()

        @pl.when(beside)
        def _():
            w_copy(q).wait_send()

        @pl.when(apart)
        def _():
            for i in range(n_mpo - 1):
                d_copy(i, q).wait_send()
            x_copy(q).wait_send()

        return carry

    lax.fori_loop(0, chunks, sent, 0)


def per_device(
    n_sec, n_mpo, two_site, left_env, right_env, left_sector, right_sector, mpo_weight, src_slot, joining
):
    blocks, blk, _ = two_site.shape
    bonds, sectors = left_env.shape[:2]
    rows = blk // n_mpo
    kb = 2
    chunks = blocks // kb
    wg = min(bonds, 16)
    pieces = 4
    peers = n_mpo - 1
    smem = pl.BlockSpec(memory_space=pltpu.SMEM)
    dma = pltpu.SemaphoreType.DMA
    f32, bf16 = jnp.float32, jnp.bfloat16
    return pl.pallas_call(
        functools.partial(kernel, n_sec, n_mpo, kb, wg),
        out_shape=jax.ShapeDtypeStruct((blocks, rows, blk), bf16),
        in_specs=[pl.BlockSpec(memory_space=pltpu.HBM)] * 3 + [smem] * 5,
        out_specs=pl.BlockSpec(memory_space=pltpu.VMEM),
        scratch_shapes=[
            pltpu.VMEM(two_site.shape, bf16),
            pltpu.VMEM(left_env.shape, bf16),
            pltpu.VMEM(right_env.shape, bf16),
            pltpu.VMEM((sectors * blk, kb * blk), bf16),
            pltpu.VMEM((blocks, blk, bonds * blk), bf16),
            pltpu.VMEM((sectors, bonds * blk, 2 * blk), bf16),
            pltpu.VMEM((sectors, bonds * blk, 2 * blk), bf16),
            pltpu.VMEM((2, blocks, blk, blk), f32),
            pltpu.VMEM((2, blocks, blk, blk), f32),
            pltpu.VMEM((peers, 2, blocks, rows, blk), f32),
            pltpu.VMEM((2, blocks, rows, blk), f32),
            pltpu.VMEM((blocks, rows, blk), f32),
            pltpu.VMEM((blocks, rows, blk), f32),
            pltpu.VMEM((blocks, blk, blk), f32),
            pltpu.VMEM((blocks, blk, blk), f32),
            pltpu.VMEM((blocks, blk, blk), f32),
            pltpu.VMEM((peers, blocks, rows, blk), f32),
            dma((PIECES + 2,)),
            dma((peers, chunks)), dma((peers, chunks)),
            dma((peers, chunks)), dma((peers, chunks)),
            dma((chunks,)), dma((chunks,)),
            dma((chunks,)), dma((chunks,)),
            dma((chunks,)), dma((chunks,)),
            dma((chunks,)), dma((chunks,)),
            dma((peers, pieces)), dma((peers, pieces)),
        ],
        compiler_params=pltpu.CompilerParams(
            collective_id=0, has_side_effects=True, vmem_limit_bytes=56 * 1024 * 1024
        ),
    )(two_site, left_env, right_env, left_sector, right_sector, mpo_weight.T, src_slot.T, joining.T)


def solution(mesh):
    placed = (
        P("sec", None, None),
        P("mpo", "sec", None, None),
        P("mpo", "sec", None, None),
        P("sec"),
        P("sec"),
        P("mpo", None),
        P("sec", None),
        P("sec", None),
    )
    return jax.shard_map(
        functools.partial(per_device, mesh.shape["sec"], mesh.shape["mpo"]),
        mesh=mesh, in_specs=placed, out_specs=P("sec", "mpo", None), check_vma=False,
    )
```
